256 devices in a mesh: blk: 32 (over x_hi, z, core), head: 8 (over y, x_lo).
Axes of the slice: x: 4 (x_hi: 2, x_lo: 2; x = x_hi * 2 + x_lo), y: 4, z: 8, core: 2. Of those that a mesh axis runs over, the one named last changes fastest.
Arguments:
- query: bfloat16 [32768, 4096], P(('blk', 'head')), may hold values from -128 to 128
- key: bfloat16 [4096, 4096], P('blk', 'head'), may hold values from -8 to 8
- value: bfloat16 [4096, 4096], P('blk', 'head'), may hold values from -6 to 6
- d_out: bfloat16 [32768, 4096], P(('blk', 'head')), may hold values from -6 to 6
- seg_map: int32 [256], replicated, may hold values from 0 to 63, never falling along the last dimension, each value on 1 to 8 neighbouring positions
- spans: int32 [64, 8], replicated, may hold values from 0 to 31, all different within a row
Outputs:
- attn_out: bfloat16 [32768, 4096], P(('blk', 'head'))
- d_query: bfloat16 [32768, 4096], P(('blk', 'head'))
- d_key: bfloat16 [4096, 4096], P('blk', 'head')
- d_value: bfloat16 [4096, 4096], P('blk', 'head')
The draws below stay inside these ranges and needn't reach their ends.
Inputs may be any that keep to these rules, and one draw needn't show every extreme that they name: `seg_map`: segment numbers never fall from one CAD block to the next; each segment covers 1 to 8 blocks, one exactly 8. `spans`: each row names 8 different document blocks; every document block is named by some row.
All inputs are finite; a program needn't handle non-finite values.
Results may differ from the reference program's by a relative error of at most 0.024.
Values may be sent and summed in bfloat16 or wider, within the bound.
No kernel may reach another device: no remote copies, remote signals or barrier semaphores. Data moves between devices by JAX's collectives and lax.ppermute only.
A program may use at most 128 MiB of HBM per device.

```python
import math
import jax
import jax.numpy as jnp
import numpy as np
from jax import lax

HEADS = 32
HEAD_DIM = 128
BLOCK = 128
SPANS = 8
CAD_TOK = 32768
DOC_TOK = 4096
ROWS_GROUP = 1024
CAD_BLOCKS = 256
DOC_BLOCKS = 32
SEGS = 64
N_BLK = 32


def draw_query(key, part):
    sample = jax.random.normal(jax.random.fold_in(key, 1), (CAD_TOK, HEADS * HEAD_DIM), jnp.float32)
    sample = jnp.clip(sample, -6.0, 6.0)
    return sample.astype(jnp.bfloat16)


def draw_key(key, part):
    sample = jax.random.normal(jax.random.fold_in(key, 2), (DOC_TOK, HEADS * HEAD_DIM), jnp.float32)
    sample = jnp.clip(sample, -6.0, 6.0)
    return sample.astype(jnp.bfloat16)


def level_of(rng, dims, shards, low, largest):
    level, own = 1.0, jax.random.fold_in(rng, 6)
    for dim, blocks in shards:
        heights = jnp.exp(jax.random.uniform(jax.random.fold_in(own, dim), (blocks,), jnp.float32, low / len(shards), largest / len(shards)))
        level = level * jnp.repeat(heights, dims[dim] // blocks).reshape([-1 if axis == dim else 1 for axis in range(len(dims))])
    return level


def picks_of(own_key, rows, amount, top, lift):
    order = jax.random.permutation(jax.random.fold_in(own_key, 1), amount)
    boost = order
    for power in range(3):
        boost = boost * boost // amount
    boost = boost * lift // amount
    chance = jax.random.randint(jax.random.fold_in(own_key, 2), (rows, amount), 0, 4096) + boost
    fixed_rows = jax.random.permutation(jax.random.fold_in(own_key, 3), rows)[jnp.arange(amount) % rows]
    chance = jnp.where(jnp.arange(rows)[:, None] == fixed_rows[None, :], 1 << 14, chance)
    score = chance * amount + jnp.arange(amount)
    return lax.top_k(score.astype(jnp.int32), top)[1].astype(jnp.int32)


def split_up(amount, total, most, slope):
    portions = [(1 << 20) // math.isqrt(grade ** slope) + 1 for grade in range(2, amount + 1)]
    surplus, counts = total - most - (amount - 1), [1] * (amount - 1)
    while surplus > 0:
        candidates = [i for i in range(amount - 1) if counts[i] < most]
        mass, left = sum([portions[i] for i in candidates]), surplus
        for i in candidates:
            extra = min(most - counts[i], max(1, left * portions[i] // mass), surplus)
            counts[i] = counts[i] + extra
            surplus = surplus - extra
    return np.array([most] + counts)


def uneven(rng, number_of, total, most, skew):
    if number_of == 2:
        one = jax.random.randint(rng, (), max(1, total - most), min(most, total - 1) + 1)
        return jnp.stack([one, total - one])
    lengths = jnp.asarray(split_up(number_of, total, most, skew), jnp.int32)
    pairs = (number_of - 1) // 2
    source_of, taker = lengths[1:1 + 2 * pairs:2], lengths[2:2 + 2 * pairs:2]
    slack = jnp.minimum(source_of - 1, most - taker)
    moved = jax.random.randint(jax.random.fold_in(rng, 1), (pairs,), 0, 1 << 20) % (slack + 1)
    lengths = lengths.at[1:1 + 2 * pairs:2].set(source_of - moved).at[2:2 + 2 * pairs:2].set(taker + moved)
    return lengths[jax.random.permutation(jax.random.fold_in(rng, 2), number_of)]


def scatter_about(key, extent, scale, limit, shards=(), kind=jnp.bfloat16):
    loudness = level_of(key, extent, shards, -0.22, 0.18) if shards else 1.0
    values = jax.random.normal(key, extent, jnp.float32) * scale * loudness
    return jnp.minimum(jnp.maximum(values, -limit), limit).astype(kind)


def setup_inputs(seed: int = 0) -> dict:
    key_of = jax.random.split(jax.random.key(seed), 7)
    query = draw_query(jax.random.fold_in(key_of[6], 71), 0)
    key = draw_key(jax.random.fold_in(key_of[6], 71), 0)
    value = scatter_about(key_of[2], (DOC_TOK, HEADS * HEAD_DIM), 1.0, 6.0, ((0, 32), (1, 8)))
    d_out = scatter_about(key_of[3], (CAD_TOK, HEADS * HEAD_DIM), 1.0, 6.0, ((0, 256),))
    seg_map = jnp.searchsorted(jnp.cumsum(uneven(key_of[4], SEGS, CAD_BLOCKS, 8, 2)), jnp.arange(CAD_BLOCKS), side="right").astype(jnp.int32)
    spans = picks_of(key_of[5], SEGS, DOC_BLOCKS, SPANS, 4096)
    return {"query": query, "key": key, "value": value, "d_out": d_out, "seg_map": seg_map, "spans": spans}


def reference(query, key, value, d_out, seg_map, spans):
    factor = 1.0 / math.sqrt(HEAD_DIM)
    group_blocks = ROWS_GROUP // BLOCK
    all_width = HEADS * HEAD_DIM
    block_ids = spans[seg_map].astype(jnp.int32)
    key_blocks = key.reshape(DOC_BLOCKS, BLOCK, HEADS, HEAD_DIM)
    value_blocks = value.reshape(DOC_BLOCKS, BLOCK, HEADS, HEAD_DIM)

    def one_group(carry, inputs):
        query_group, dout_group, group_ids = inputs
        query_four = query_group.reshape(group_blocks, BLOCK, HEADS, HEAD_DIM).astype(jnp.float32)
        dout_four = dout_group.reshape(group_blocks, BLOCK, HEADS, HEAD_DIM).astype(jnp.float32)
        key_tiles = key_blocks[group_ids].reshape(group_blocks, SPANS * BLOCK, HEADS, HEAD_DIM).astype(jnp.float32)
        value_tiles = value_blocks[group_ids].reshape(group_blocks, SPANS * BLOCK, HEADS, HEAD_DIM).astype(jnp.float32)
        scores = jnp.einsum('cqhd,ckhd->chqk', query_four, key_tiles) * factor
        top_score = lax.optimization_barrier(jnp.max(scores, axis=-1, keepdims=True))
        expo = jnp.exp(scores - top_score)
        prob = expo / lax.optimization_barrier(jnp.sum(expo, axis=-1, keepdims=True))
        prob_b = prob.astype(jnp.bfloat16).astype(jnp.float32)
        attn = jnp.einsum('chqk,ckhd->cqhd', prob_b, value_tiles)
        delta = lax.optimization_barrier(jnp.sum(dout_four * attn, axis=-1))
        delta = jnp.transpose(delta, (0, 2, 1))[..., None]
        dprob = jnp.einsum('cqhd,ckhd->chqk', dout_four, value_tiles)
        dscore_b = (prob * (dprob - delta)).astype(jnp.bfloat16).astype(jnp.float32)
        grad_query = (jnp.einsum('chqk,ckhd->cqhd', dscore_b, key_tiles) * factor).astype(jnp.bfloat16)
        key_slots = jnp.einsum('chqk,cqhd->ckhd', dscore_b, query_four) * factor
        value_slots = jnp.einsum('chqk,cqhd->ckhd', prob_b, dout_four)
        flat_ids = group_ids.reshape(group_blocks * SPANS)
        key_sum = carry[0].at[flat_ids].add(key_slots.reshape(group_blocks * SPANS, BLOCK, all_width))
        value_sum = carry[1].at[flat_ids].add(value_slots.reshape(group_blocks * SPANS, BLOCK, all_width))
        outputs = (attn.astype(jnp.bfloat16).reshape(ROWS_GROUP, all_width), grad_query.reshape(ROWS_GROUP, all_width))
        return ((key_sum, value_sum), outputs)
    start_sums = (jnp.zeros((DOC_BLOCKS, BLOCK, all_width), jnp.float32), jnp.zeros((DOC_BLOCKS, BLOCK, all_width), jnp.float32))
    inputs = (query.reshape(N_BLK, ROWS_GROUP, all_width), d_out.reshape(N_BLK, ROWS_GROUP, all_width), block_ids.reshape(N_BLK, group_blocks, SPANS))
    (key_sum, value_sum), (attn_all, grad_all) = lax.scan(one_group, start_sums, inputs)
    attn_out = attn_all.reshape(CAD_TOK, all_width)
    d_query = grad_all.reshape(CAD_TOK, all_width)
    d_key = key_sum.reshape(DOC_TOK, all_width).astype(jnp.bfloat16)
    d_value = value_sum.reshape(DOC_TOK, all_width).astype(jnp.bfloat16)
    return (attn_out, d_query, d_key, d_value)
```

```python
import functools
import math

import jax
import jax.numpy as jnp
from jax import lax
from jax.experimental import pallas as pl
from jax.experimental.pallas import tpu as pltpu
from jax.sharding import Mesh, PartitionSpec as P

HEAD_DIM = 128
BLOCK = 128
SPANS = 8
PLANE = ("head", "xhi", "core")
FACTOR = 1.0 / math.sqrt(HEAD_DIM)
LOG2E = math.log2(math.e)
UNROLL = 2


def nt(a, b):
    return lax.dot_general(a, b, (((1,), (1,)), ((), ())), preferred_element_type=jnp.float32)


def nn(a, b):
    return lax.dot_general(a, b, (((1,), (0,)), ((), ())), preferred_element_type=jnp.float32)


def attention_kernel(
    zi_ref, seg_ref, spans_ref, q_ref, do_ref, kv_ref, o_ref, dq_ref, dkv_ref, kvt_ref, acc_ref
):
    z = zi_ref[0]
    doc_blocks = kv_ref.shape[0]
    cad_blocks = q_ref.shape[0]

    @pl.loop(0, doc_blocks)
    def _(d):
        tile = kv_ref[d]
        kvt_ref[d, :HEAD_DIM, :] = tile[:, :HEAD_DIM].T
        kvt_ref[d, HEAD_DIM:, :] = tile[:, HEAD_DIM:].T
        acc_ref[d] = jnp.zeros(acc_ref.shape[1:], jnp.float32)

    zero = jnp.zeros((BLOCK, HEAD_DIM), jnp.bfloat16)

    def one_block(s):
        head, xhi, core = s // 4, (s // 2) % 2, s % 2
        seg = seg_ref[(xhi * 16 + z * 2 + core) * 8 + head]
        locs = []
        for j in range(SPANS):
            d = spans_ref[j, seg]
            locs.append(((d // 2) % 8) * 4 + (d // 16) * 2 + d % 2)
        q, do = q_ref[s], do_ref[s]
        diag = jnp.concatenate(
            [jnp.concatenate([q, zero], axis=1), jnp.concatenate([zero, do], axis=1)], axis=0
        )
        kv = jnp.concatenate([kv_ref[loc] for loc in locs], axis=0)
        both = nt(kv, diag)
        scores, dprob = both[:, :BLOCK], both[:, BLOCK:]
        top = jnp.max(scores, axis=0, keepdims=True)
        expo = jnp.exp2((scores - top) * (FACTOR * LOG2E))
        prob = expo * (1.0 / jnp.sum(expo, axis=0, keepdims=True))
        prob_b = prob.astype(jnp.bfloat16)
        value_t = jnp.concatenate([kvt_ref[loc, HEAD_DIM:, :] for loc in locs], axis=1)
        attn_t = nn(value_t, prob_b)
        attn = attn_t.T
        o_ref[s] = attn.astype(jnp.bfloat16)
        delta = jnp.sum(do.astype(jnp.float32).T * attn_t, axis=0, keepdims=True)
        dscore_b = (prob * (dprob - delta)).astype(jnp.bfloat16)
        key_t = jnp.concatenate([kvt_ref[loc, :HEAD_DIM, :] for loc in locs], axis=1)
        dq_t = nn(key_t, dscore_b) * FACTOR
        dq_ref[s] = dq_t.T.astype(jnp.bfloat16)
        slots = nn(jnp.concatenate([dscore_b, prob_b], axis=1), diag)
        for j in range(SPANS):
            acc_ref[locs[j]] += slots[j * BLOCK : (j + 1) * BLOCK]

    @pl.loop(0, cad_blocks // UNROLL)
    def _(i):
        for u in range(UNROLL):
            one_block(i * UNROLL + u)

    @pl.loop(0, doc_blocks)
    def _(d):
        dkv_ref[d, :, :HEAD_DIM] = (acc_ref[d, :, :HEAD_DIM] * FACTOR).astype(jnp.bfloat16)
        dkv_ref[d, :, HEAD_DIM:] = acc_ref[d, :, HEAD_DIM:].astype(jnp.bfloat16)


def attention(zi, seg_map, spans_t, q, do, kv):
    cad_blocks, doc_blocks = q.shape[0], kv.shape[0]
    smem = pl.BlockSpec(memory_space=pltpu.SMEM)
    vmem = pl.BlockSpec(memory_space=pltpu.VMEM)
    return pl.pallas_call(
        attention_kernel,
        out_shape=(
            jax.ShapeDtypeStruct(q.shape, jnp.bfloat16),
            jax.ShapeDtypeStruct(q.shape, jnp.bfloat16),
            jax.ShapeDtypeStruct(kv.shape, jnp.bfloat16),
        ),
        in_specs=[smem, smem, smem, vmem, vmem, vmem],
        out_specs=(vmem, vmem, vmem),
        scratch_shapes=[
            pltpu.VMEM((doc_blocks, 2 * HEAD_DIM, BLOCK), jnp.bfloat16),
            pltpu.VMEM((doc_blocks, BLOCK, 2 * HEAD_DIM), jnp.float32),
        ],
        compiler_params=pltpu.CompilerParams(vmem_limit_bytes=48 * 2**20),
        cost_estimate=pl.CostEstimate(
            flops=cad_blocks * SPANS * 12 * BLOCK * BLOCK * HEAD_DIM,
            bytes_accessed=2 * (4 * q.size + 2 * kv.size),
            transcendentals=cad_blocks * SPANS * BLOCK * BLOCK,
        ),
        name="attention",
    )(zi, seg_map, spans_t, q, do, kv)


def swap(array, axes):
    return lax.all_to_all(array, axes, split_axis=0, concat_axis=0, tiled=True)


def body(query, key, value, d_out, seg_map, spans):
    rows = query.shape[0]

    def by_head(array):
        return array.reshape(rows, -1, HEAD_DIM).transpose(1, 0, 2)

    kv = swap(jnp.concatenate([by_head(key), by_head(value)], axis=2), ("xhi", "core"))
    kv = lax.all_gather(kv, "z", axis=0, tiled=True)
    q = swap(by_head(query), PLANE)
    do = swap(by_head(d_out), PLANE)
    zi = lax.axis_index("z").astype(jnp.int32).reshape(1)
    o, dq, dkv = attention(zi, seg_map, spans.T, q, do, kv)
    dkv = lax.psum_scatter(dkv, "z", scatter_dimension=0, tiled=True)
    o, dq = swap(o, PLANE), swap(dq, PLANE)
    dkv = swap(dkv, ("xhi", "core"))

    def by_rows(array):
        return array.transpose(1, 0, 2).reshape(rows, -1)

    return (
        by_rows(o),
        by_rows(dq),
        by_rows(dkv[:, :, :HEAD_DIM]),
        by_rows(dkv[:, :, HEAD_DIM:]),
    )


def solution(mesh):
    fine = Mesh(mesh.devices.reshape(2, 8, 2, 8), ("xhi", "z", "core", "head"))
    blk = ("xhi", "z", "core")
    rows, tiles = P((*blk, "head"), None), P(blk, "head")
    return jax.shard_map(
        body,
        mesh=fine,
        in_specs=(rows, tiles, tiles, rows, P(), P()),
        out_specs=(rows, rows, tiles, tiles),
        check_vma=False,
    )
```

```python
import math

import jax
import jax.numpy as jnp
from jax import lax
from jax.experimental import pallas as pl
from jax.experimental.pallas import tpu as pltpu
from jax.sharding import Mesh, PartitionSpec as P

HEAD_DIM = 128
BLOCK = 128
SPANS = 8
PLANES = 8
PLANE = ("head", "xhi", "core")
QUAD = ("xhi", "core")
FACTOR = 1.0 / math.sqrt(HEAD_DIM)
LOG2E = math.log2(math.e)
UNROLL = 4
VMEM_MIB = 8
BIG_MIB = 60
WIDE = 2 * HEAD_DIM
BF16, F32 = jnp.bfloat16, jnp.float32
SMEM = pl.BlockSpec(memory_space=pltpu.SMEM)
VMEM = pl.BlockSpec(memory_space=pltpu.VMEM)


def nt(a, b):
    return lax.dot_general(a, b, (((1,), (1,)), ((), ())), preferred_element_type=F32)


def nn(a, b):
    return lax.dot_general(a, b, (((1,), (0,)), ((), ())), preferred_element_type=F32)


def columns(block):
    return pl.ds(pl.multiple_of(block * HEAD_DIM, HEAD_DIM), HEAD_DIM)


def call(kernel, name, in_specs, shapes, scratch=(), **params):
    return pl.pallas_call(
        kernel,
        out_shape=tuple(jax.ShapeDtypeStruct(shape, BF16) for shape in shapes),
        in_specs=in_specs,
        out_specs=tuple(VMEM for _ in shapes),
        scratch_shapes=scratch,
        name=name,
        compiler_params=pltpu.CompilerParams(vmem_limit_bytes=(BIG_MIB if name == 'attention' else VMEM_MIB) * 2**20),
        **params,
    )


def split_kv(me, key, value):
    def kernel(me_ref, key_ref, value_ref, *tiles):
        for t, tile in enumerate(tiles):
            tile[:, :HEAD_DIM] = key_ref[:, columns(me_ref[0] ^ t)]
            tile[:, HEAD_DIM:] = value_ref[:, columns(me_ref[0] ^ t)]

    return call(kernel, "split_kv", [SMEM, VMEM, VMEM], [(BLOCK, WIDE)] * 4)(me, key, value)


def join_kv(me, tiles):
    def kernel(me_ref, *refs):
        *tiles, key_ref, value_ref = refs
        for t, tile in enumerate(tiles):
            key_ref[:, columns(me_ref[0] ^ t)] = tile[:, :HEAD_DIM]
            value_ref[:, columns(me_ref[0] ^ t)] = tile[:, HEAD_DIM:]

    return call(kernel, "join_kv", [SMEM] + [VMEM] * 4, [(BLOCK, 4 * HEAD_DIM)] * 2)(me, *tiles)


def split_heads(query, d_out):
    heads = query.shape[1] // HEAD_DIM

    def kernel(query_ref, d_out_ref, tiles):
        for h in range(heads):
            tiles[h, :, :HEAD_DIM] = query_ref[:, columns(h)]
            tiles[h, :, HEAD_DIM:] = d_out_ref[:, columns(h)]

    return call(kernel, "split_heads", [VMEM] * 2, [(heads, BLOCK, WIDE)])(query, d_out)[0]


def join_heads(tiles):
    heads = tiles.shape[0]

    def kernel(tiles, attn_ref, grad_ref):
        for h in range(heads):
            attn_ref[:, columns(h)] = tiles[h, :, :HEAD_DIM]
            grad_ref[:, columns(h)] = tiles[h, :, HEAD_DIM:]

    return call(kernel, "join_heads", [VMEM], [(BLOCK, heads * HEAD_DIM)] * 2)(tiles)


def plus(*terms):
    return sum(term.astype(F32) for term in terms).astype(BF16)


def attention_kernel(me_ref, seg_ref, spans_ref, qd_ref, *refs):
    pieces, (od_ref, *parts), (kv_ref, kvt_ref, acc_ref) = refs[:9], refs[9:19], refs[19:]
    quad, z = me_ref[0], me_ref[1]
    cad_blocks = qd_ref.shape[0]

    def places(first):
        own, up1, down1, up2, down2, up3, down3, up4, down4 = first
        return (
            (own, 0), (down1, 1), (down2, 2), (down3, 3), (up3, 5), (up2, 6), (up1, 7)
        ), (up4, down4)

    whole, halves = places(pieces)
    for piece, at in (*((p, 4 * o) for p, o in whole), (halves[0], 16), (halves[1], 18)):

        @pl.loop(0, piece.shape[0])
        def _(t):
            tile = piece[t]
            kv_ref[at + t] = tile
            kvt_ref[at + t, :HEAD_DIM, :] = tile[:, :HEAD_DIM].T
            kvt_ref[at + t, HEAD_DIM:, :] = tile[:, HEAD_DIM:].T
            acc_ref[at + t] = jnp.zeros((BLOCK, WIDE), F32)

    def one_block(s):
        head, xhi, core = s // 4, (s // 2) % 2, s % 2
        seg = seg_ref[(xhi * 16 + z * 2 + core) * 8 + head]
        locs = []
        for j in range(SPANS):
            d = spans_ref[j, seg]
            away = ((d // 2) % 8 - z) & 7
            locs.append(away * 4 + (((d // 16) * 2 + d % 2) ^ quad))
        q, do = qd_ref[s, :, :HEAD_DIM], qd_ref[s, :, HEAD_DIM:]
        keys = jnp.concatenate([kv_ref[loc, :, :HEAD_DIM] for loc in locs], axis=0)
        scores = nt(keys, q)
        top = jnp.max(scores, axis=0, keepdims=True)
        expo = jnp.exp2((scores - top) * (FACTOR * LOG2E))
        prob = expo * (1.0 / jnp.sum(expo, axis=0, keepdims=True))
        prob_b = prob.astype(BF16)
        value_t = jnp.concatenate([kvt_ref[loc, HEAD_DIM:, :] for loc in locs], axis=1)
        attn_t = nn(value_t, prob_b)
        od_ref[s, :, :HEAD_DIM] = attn_t.T.astype(BF16)
        values = jnp.concatenate([kv_ref[loc, :, HEAD_DIM:] for loc in locs], axis=0)
        dprob = nt(values, do)
        delta = jnp.sum(do.astype(F32).T * attn_t, axis=0, keepdims=True)
        dscore_b = (prob * (dprob - delta)).astype(BF16)
        key_t = jnp.concatenate([kvt_ref[loc, :HEAD_DIM, :] for loc in locs], axis=1)
        dq_t = nn(key_t, dscore_b) * FACTOR
        od_ref[s, :, HEAD_DIM:] = dq_t.T.astype(BF16)
        key_slots, value_slots = nn(dscore_b, q), nn(prob_b, do)
        for j in range(SPANS):
            rows = slice(j * BLOCK, (j + 1) * BLOCK)
            acc_ref[locs[j], :, :HEAD_DIM] += key_slots[rows]
            acc_ref[locs[j], :, HEAD_DIM:] += value_slots[rows]

    @pl.loop(0, cad_blocks // UNROLL)
    def _(i):
        for u in range(UNROLL):
            one_block(i * UNROLL + u)

    own, up1, up2, up3, up4, down1, down2, down3, down4 = parts
    for part, at in (
        (own, 0), (up1, 4), (up2, 8), (up3, 12), (up4, 16),
        (down4, 18), (down3, 20), (down2, 24), (down1, 28),
    ):

        @pl.loop(0, part.shape[0])
        def _(t):
            part[t, :, :HEAD_DIM] = (acc_ref[at + t, :, :HEAD_DIM] * FACTOR).astype(BF16)
            part[t, :, HEAD_DIM:] = acc_ref[at + t, :, HEAD_DIM:].astype(BF16)


def attention(me, seg_map, spans_t, qd, pieces):
    cad_blocks, doc_blocks = qd.shape[0], 4 * PLANES
    whole, half = (4, BLOCK, WIDE), (2, BLOCK, WIDE)
    return call(
        attention_kernel,
        "attention",
        [SMEM] * 3 + [VMEM] * 10,
        [qd.shape] + ([whole] * 4 + [half] + [whole] * 3 + [half]),
        [
            pltpu.VMEM((doc_blocks, BLOCK, WIDE), BF16),
            pltpu.VMEM((doc_blocks, WIDE, BLOCK), BF16),
            pltpu.VMEM((doc_blocks, BLOCK, WIDE), F32),
        ],
        cost_estimate=pl.CostEstimate(
            flops=cad_blocks * SPANS * 12 * BLOCK * BLOCK * HEAD_DIM,
            bytes_accessed=2 * (2 * qd.size + 2 * doc_blocks * BLOCK * WIDE),
            transcendentals=cad_blocks * SPANS * BLOCK * BLOCK,
        ),
    )(me, seg_map, spans_t, qd, *pieces)


def up(array):
    return lax.ppermute(array, "z", [(i, (i + 1) % PLANES) for i in range(PLANES)])


def down(array):
    return lax.ppermute(array, "z", [(i, (i - 1) % PLANES) for i in range(PLANES)])


def exchange(tiles):
    return [tiles[0]] + [
        lax.ppermute(tiles[t], QUAD, [(i, i ^ t) for i in range(4)]) for t in (1, 2, 3)
    ]


def gather_z(own):
    up1, down1 = up(own), down(own)
    up2, down2 = up(up1), down(down1)
    up3, down3 = up(up2), down(down2)
    up4, down4 = up(up3[:2]), down(down3[2:])
    return own, up1, down1, up2, down2, up3, down3, up4, down4


def scatter_z(parts, beside):
    own, up1, up2, up3, up4, down1, down2, down3, down4 = parts
    ups, downs = up(up4), down(down4)
    beside, ups, downs = lax.optimization_barrier((beside, ups, downs))
    beside = swap(beside)
    ups = up(jnp.concatenate([plus(up3[:2], ups), up3[2:]]))
    downs = down(jnp.concatenate([down3[:2], plus(down3[2:], downs)]))
    ups, downs = up(plus(up2, ups)), down(plus(down2, downs))
    ups, downs = up(plus(up1, ups)), down(plus(down1, downs))
    beside, ups, downs = lax.optimization_barrier((beside, ups, downs))
    return [plus(own[t], ups[t], downs[t]) for t in range(4)], beside


def swap(array):
    return lax.all_to_all(array, PLANE, split_axis=0, concat_axis=0, tiled=True)


def body(query, key, value, d_out, seg_map, spans):
    me = jnp.stack([lax.axis_index(QUAD), lax.axis_index("z")]).astype(jnp.int32)
    tiles = exchange(split_kv(me, key, value))
    qd, tiles = lax.optimization_barrier((split_heads(query, d_out), tiles))
    qd, pieces = swap(qd), gather_z(jnp.stack(tiles))
    od, *parts = attention(me, seg_map, spans.T, qd, pieces)
    tiles, od = scatter_z(parts, od)
    attn_out, d_query = join_heads(od)
    d_key, d_value = join_kv(me, exchange(tiles))
    return attn_out, d_query, d_key, d_value


def solution(mesh):
    fine = Mesh(mesh.devices.reshape(2, PLANES, 2, 8), ("xhi", "z", "core", "head"))
    blk = ("xhi", "z", "core")
    rows, tiles = P((*blk, "head"), None), P(blk, "head")
    return jax.shard_map(
        body,
        mesh=fine,
        in_specs=(rows, tiles, tiles, rows, P(), P()),
        out_specs=(rows, rows, tiles, tiles),
        check_vma=False,
    )
```

```python
import math

import jax
import jax.numpy as jnp
from jax import lax
from jax.experimental import pallas as pl
from jax.experimental.pallas import tpu as pltpu
from jax.sharding import Mesh, PartitionSpec as P

HEAD_DIM = 128
BLOCK = 128
SPANS = 8
PLANES = 8
PLANE = ("head", "xhi", "core")
QUAD = ("xhi", "core")
FACTOR = 1.0 / math.sqrt(HEAD_DIM)
LOG2E = math.log2(math.e)
UNROLL = 8
VMEM_MIB = 8
BIG_MIB = 60
WIDE = 2 * HEAD_DIM
BF16, F32 = jnp.bfloat16, jnp.float32
SMEM = pl.BlockSpec(memory_space=pltpu.SMEM)
VMEM = pl.BlockSpec(memory_space=pltpu.VMEM)


def nt(a, b):
    return lax.dot_general(a, b, (((1,), (1,)), ((), ())), preferred_element_type=F32)


def nn(a, b):
    return lax.dot_general(a, b, (((1,), (0,)), ((), ())), preferred_element_type=F32)


def columns(block):
    return pl.ds(pl.multiple_of(block * HEAD_DIM, HEAD_DIM), HEAD_DIM)


def call(kernel, name, in_specs, shapes, scratch=(), out_specs=None, **params):
    return pl.pallas_call(
        kernel,
        out_shape=tuple(jax.ShapeDtypeStruct(shape, BF16) for shape in shapes),
        in_specs=in_specs,
        out_specs=tuple(out_specs or [VMEM for _ in shapes]),
        scratch_shapes=scratch,
        name=name,
        compiler_params=pltpu.CompilerParams(vmem_limit_bytes=(BIG_MIB if name == 'attention' else VMEM_MIB) * 2**20),
        **params,
    )


def split_kv(me, key, value):
    def kernel(me_ref, key_ref, value_ref, *tiles):
        for t, tile in enumerate(tiles):
            tile[:, :HEAD_DIM] = key_ref[:, columns(me_ref[0] ^ t)]
            tile[:, HEAD_DIM:] = value_ref[:, columns(me_ref[0] ^ t)]

    return call(kernel, "split_kv", [SMEM, VMEM, VMEM], [(BLOCK, WIDE)] * 4)(me, key, value)


def join_kv(me, tiles):
    def kernel(me_ref, *refs):
        *tiles, key_ref, value_ref = refs
        for t, tile in enumerate(tiles):
            key_ref[:, columns(me_ref[0] ^ t)] = tile[:, :HEAD_DIM]
            value_ref[:, columns(me_ref[0] ^ t)] = tile[:, HEAD_DIM:]

    return call(kernel, "join_kv", [SMEM] + [VMEM] * 4, [(BLOCK, 4 * HEAD_DIM)] * 2)(me, *tiles)


def split_heads(query, d_out):
    heads = query.shape[1] // HEAD_DIM

    def kernel(query_ref, d_out_ref, tiles):
        for h in range(heads):
            tiles[h, :, :HEAD_DIM] = query_ref[:, columns(h)]
            tiles[h, :, HEAD_DIM:] = d_out_ref[:, columns(h)]

    return call(kernel, "split_heads", [VMEM] * 2, [(heads, BLOCK, WIDE)])(query, d_out)[0]


def join_heads(tiles):
    heads = tiles.shape[0]

    def kernel(tiles, attn_ref, grad_ref):
        for h in range(heads):
            attn_ref[:, columns(h)] = tiles[h, :, :HEAD_DIM]
            grad_ref[:, columns(h)] = tiles[h, :, HEAD_DIM:]

    return call(kernel, "join_heads", [VMEM], [(BLOCK, heads * HEAD_DIM)] * 2)(tiles)


def plus(*terms):
    return sum(term.astype(F32) for term in terms).astype(BF16)


def attention_kernel(me_ref, seg_ref, spans_ref, qd_ref, *refs):
    pieces, (od_ref, *parts), (kv_ref, kvt_ref, acc_ref) = refs[:9], refs[9:19], refs[19:]
    quad, z = me_ref[0], me_ref[1]

    @pl.when(pl.program_id(0) == 0)
    def _():
        own, up1, down1, up2, down2, up3, down3, up4, down4 = pieces
        for piece, at in (
            (own, 0), (down1, 4), (down2, 8), (down3, 12), (up4, 16),
            (down4, 18), (up3, 20), (up2, 24), (up1, 28),
        ):

            @pl.loop(0, piece.shape[0], unroll=True)
            def _(t):
                tile = piece[t]
                kv_ref[at + t] = tile
                kvt_ref[at + t, :HEAD_DIM, :] = tile[:, :HEAD_DIM].T
                kvt_ref[at + t, HEAD_DIM:, :] = tile[:, HEAD_DIM:].T
                acc_ref[at + t] = jnp.zeros((BLOCK, WIDE), F32)

    def one_block(u):
        s = pl.program_id(0) * UNROLL + u
        head, xhi, core = s // 4, (s // 2) % 2, s % 2
        seg = seg_ref[(xhi * 16 + z * 2 + core) * 8 + head]
        locs = []
        for j in range(SPANS):
            d = spans_ref[j, seg]
            away = ((d // 2) % 8 - z) & 7
            locs.append(away * 4 + (((d // 16) * 2 + d % 2) ^ quad))
        q, do = qd_ref[u, :, :HEAD_DIM], qd_ref[u, :, HEAD_DIM:]
        keys = jnp.concatenate([kv_ref[loc, :, :HEAD_DIM] for loc in locs], axis=0)
        scores = nt(keys, q)
        values = jnp.concatenate([kv_ref[loc, :, HEAD_DIM:] for loc in locs], axis=0)
        yield
        dprob = nt(values, do)
        top = jnp.max(scores, axis=0, keepdims=True)
        expo = jnp.exp2((scores - top) * (FACTOR * LOG2E))
        prob = expo * (1.0 / jnp.sum(expo, axis=0, keepdims=True))
        prob_b = prob.astype(BF16)
        value_t = jnp.concatenate([kvt_ref[loc, HEAD_DIM:, :] for loc in locs], axis=1)
        yield
        attn_t = nn(value_t, prob_b)
        yield
        value_slots = nn(prob_b, do)
        od_ref[u, :, :HEAD_DIM] = attn_t.T.astype(BF16)
        delta = jnp.sum(do.astype(F32).T * attn_t, axis=0, keepdims=True)
        dscore_b = (prob * (dprob - delta)).astype(BF16)
        key_t = jnp.concatenate([kvt_ref[loc, :HEAD_DIM, :] for loc in locs], axis=1)
        yield
        dq_t = nn(key_t, dscore_b) * FACTOR
        key_slots = nn(dscore_b, q)
        yield
        od_ref[u, :, HEAD_DIM:] = dq_t.T.astype(BF16)
        for j in range(SPANS):
            rows = slice(j * BLOCK, (j + 1) * BLOCK)
            acc_ref[locs[j], :, :HEAD_DIM] += key_slots[rows]
            acc_ref[locs[j], :, HEAD_DIM:] += value_slots[rows]

    live = [one_block(u) for u in range(UNROLL)]
    while live:
        live = [block for block in live if next(block, True) is None]

    @pl.when(pl.program_id(0) == pl.num_programs(0) - 1)
    def _():
        own, up1, up2, up3, up4, down1, down2, down3, down4 = parts
        for part, at in (
            (own, 0), (up1, 4), (up2, 8), (up3, 12), (up4, 16),
            (down4, 18), (down3, 20), (down2, 24), (down1, 28),
        ):

            @pl.loop(0, part.shape[0])
            def _(t):
                part[t, :, :HEAD_DIM] = (acc_ref[at + t, :, :HEAD_DIM] * FACTOR).astype(BF16)
                part[t, :, HEAD_DIM:] = acc_ref[at + t, :, HEAD_DIM:].astype(BF16)


def attention(me, seg_map, spans_t, qd, pieces):
    cad_blocks, doc_blocks = qd.shape[0], 4 * PLANES
    step = pl.BlockSpec((UNROLL, BLOCK, WIDE), lambda i: (i, 0, 0))
    whole, half = (4, BLOCK, WIDE), (2, BLOCK, WIDE)
    parts = [whole] * 4 + [half] + [whole] * 3 + [half]
    return call(
        attention_kernel,
        "attention",
        [SMEM] * 3 + [step] + [VMEM] * 9,
        [qd.shape] + parts,
        [
            pltpu.VMEM((doc_blocks, BLOCK, WIDE), BF16),
            pltpu.VMEM((doc_blocks, WIDE, BLOCK), BF16),
            pltpu.VMEM((doc_blocks, BLOCK, WIDE), F32),
        ],
        [step] + [VMEM] * 9,
        grid=(cad_blocks // UNROLL,),
        cost_estimate=pl.CostEstimate(
            flops=cad_blocks * SPANS * 12 * BLOCK * BLOCK * HEAD_DIM,
            bytes_accessed=2 * (2 * qd.size + 2 * doc_blocks * BLOCK * WIDE),
            transcendentals=cad_blocks * SPANS * BLOCK * BLOCK,
        ),
    )(me, seg_map, spans_t, qd, *pieces)


def up(array):
    return lax.ppermute(array, "z", [(i, (i + 1) % PLANES) for i in range(PLANES)])


def down(array):
    return lax.ppermute(array, "z", [(i, (i - 1) % PLANES) for i in range(PLANES)])


def exchange(tiles):
    return [tiles[0]] + [
        lax.ppermute(tiles[t], QUAD, [(i, i ^ t) for i in range(4)]) for t in (1, 2, 3)
    ]


def gather_z(own, up1, down1):
    up2, down2 = up(up1), down(down1)
    up3, down3 = up(up2), down(down2)
    up4, down4 = up(up3[:2]), down(down3[2:])
    return own, up1, down1, up2, down2, up3, down3, up4, down4


def scatter_z(parts, beside):
    own, up1, up2, up3, up4, down1, down2, down3, down4 = parts
    ups, downs = up(up4), down(down4)
    beside = swap(beside)
    ups = up(jnp.concatenate([plus(up3[:2], ups), up3[2:]]))
    downs = down(jnp.concatenate([down3[:2], plus(down3[2:], downs)]))
    ups, downs = up(plus(up2, ups)), down(plus(down2, downs))
    ups, downs = up(plus(up1, ups)), down(plus(down1, downs))
    beside, ups, downs = lax.optimization_barrier((beside, ups, downs))
    return [plus(own[t], ups[t], downs[t]) for t in range(4)], beside


def swap(array):
    return lax.all_to_all(array, PLANE, split_axis=0, concat_axis=0, tiled=True)


def body(query, key, value, d_out, seg_map, spans):
    me = jnp.stack([lax.axis_index(QUAD), lax.axis_index("z")]).astype(jnp.int32)
    tiles = exchange(split_kv(me, key, value))
    qd, tiles = lax.optimization_barrier((split_heads(query, d_out), tiles))
    kv = jnp.stack(tiles)
    qd, pieces = swap(qd), gather_z(kv, up(kv), down(kv))
    od, *parts = attention(me, seg_map, spans.T, qd, pieces)
    tiles, od = scatter_z(parts, od)
    attn_out, d_query = join_heads(od)
    d_key, d_value = join_kv(me, exchange(tiles))
    return attn_out, d_query, d_key, d_value


def solution(mesh):
    fine = Mesh(mesh.devices.reshape(2, PLANES, 2, 8), ("xhi", "z", "core", "head"))
    blk = ("xhi", "z", "core")
    rows, tiles = P((*blk, "head"), None), P(blk, "head")
    return jax.shard_map(
        body,
        mesh=fine,
        in_specs=(rows, tiles, tiles, rows, P(), P()),
        out_specs=(rows, rows, tiles, tiles),
        check_vma=False,
    )
```

```python
import math

import jax
import jax.numpy as jnp
from jax import lax
from jax.experimental import pallas as pl
from jax.experimental.pallas import tpu as pltpu
from jax.sharding import Mesh, PartitionSpec as P

HEAD_DIM = 128
BLOCK = 128
SPANS = 8
PLANES = 8
PLANE = ("head", "xhi", "core")
QUAD = ("xhi", "core")
FACTOR = 1.0 / math.sqrt(HEAD_DIM)
LOG2E = math.log2(math.e)
UNROLL = 8
VMEM_MIB, SMALL_MIB = 60, 8
WIDE = 2 * HEAD_DIM
BF16, F32 = jnp.bfloat16, jnp.float32
SMEM = pl.BlockSpec(memory_space=pltpu.SMEM)
VMEM = pl.BlockSpec(memory_space=pltpu.VMEM)


def nt(a, b):
    return lax.dot_general(a, b, (((1,), (1,)), ((), ())), preferred_element_type=F32)


def nn(a, b):
    return lax.dot_general(a, b, (((1,), (0,)), ((), ())), preferred_element_type=F32)


def columns(block):
    return pl.ds(pl.multiple_of(block * HEAD_DIM, HEAD_DIM), HEAD_DIM)


def call(kernel, name, in_specs, shapes, scratch=(), out_specs=None, **params):
    return pl.pallas_call(
        kernel,
        out_shape=tuple(jax.ShapeDtypeStruct(shape, BF16) for shape in shapes),
        in_specs=in_specs,
        out_specs=tuple(out_specs or [VMEM for _ in shapes]),
        scratch_shapes=scratch,
        name=name,
        compiler_params=pltpu.CompilerParams(vmem_limit_bytes=(SMALL_MIB if name.startswith("join") else VMEM_MIB) * 2**20),
        **params,
    )


def split_kv(me, key, value):
    def kernel(me_ref, key_ref, value_ref, *tiles):
        for t, tile in enumerate(tiles):
            tile[:, :HEAD_DIM] = key_ref[:, columns(me_ref[0] ^ t)]
            tile[:, HEAD_DIM:] = value_ref[:, columns(me_ref[0] ^ t)]

    return call(kernel, "split_kv", [SMEM, VMEM, VMEM], [(BLOCK, WIDE)] * 4)(me, key, value)


def join_kv(me, tiles):
    def kernel(me_ref, *refs):
        *tiles, key_ref, value_ref = refs
        for t, tile in enumerate(tiles):
            key_ref[:, columns(me_ref[0] ^ t)] = tile[:, :HEAD_DIM]
            value_ref[:, columns(me_ref[0] ^ t)] = tile[:, HEAD_DIM:]

    return call(kernel, "join_kv", [SMEM] + [VMEM] * 4, [(BLOCK, 4 * HEAD_DIM)] * 2)(me, *tiles)


def split_heads(query, d_out):
    heads = query.shape[1] // HEAD_DIM

    def kernel(query_ref, d_out_ref, tiles):
        for h in range(heads):
            tiles[h, :, :HEAD_DIM] = query_ref[:, columns(h)]
            tiles[h, :, HEAD_DIM:] = d_out_ref[:, columns(h)]

    return call(kernel, "split_heads", [VMEM] * 2, [(heads, BLOCK, WIDE)])(query, d_out)[0]


def join_heads(tiles):
    heads = tiles.shape[0]

    def kernel(tiles, attn_ref, grad_ref):
        for h in range(heads):
            attn_ref[:, columns(h)] = tiles[h, :, :HEAD_DIM]
            grad_ref[:, columns(h)] = tiles[h, :, HEAD_DIM:]

    return call(kernel, "join_heads", [VMEM], [(BLOCK, heads * HEAD_DIM)] * 2)(tiles)


def plus(*terms):
    return sum(term.astype(F32) for term in terms).astype(BF16)


def attention_kernel(me_ref, seg_ref, spans_ref, qd_ref, *refs):
    keys_in, values_in, od_ref = refs[:PLANES], refs[PLANES : 2 * PLANES], refs[2 * PLANES]
    key_parts, value_parts = refs[2 * PLANES + 1 : 3 * PLANES + 1], refs[3 * PLANES + 1 : 4 * PLANES + 1]
    k_ref, v_ref, kt_ref, vt_ref, dk_ref, dv_ref = refs[4 * PLANES + 1 :]
    quad, z = me_ref[0], me_ref[1]

    @pl.when(pl.program_id(0) == 0)
    def _():
        for o in range(PLANES):

            @pl.loop(0, 4, unroll=True)
            def _(t):
                for piece, held, turned, total in (
                    (keys_in[o], k_ref, kt_ref, dk_ref),
                    (values_in[o], v_ref, vt_ref, dv_ref),
                ):
                    tile = piece[t]
                    held[4 * o + t] = tile
                    turned[4 * o + t] = tile.T
                    total[4 * o + t] = jnp.zeros((BLOCK, HEAD_DIM), F32)

    def one_block(u):
        s = pl.program_id(0) * UNROLL + u
        head, xhi, core = s // 4, (s // 2) % 2, s % 2
        seg = seg_ref[(xhi * 16 + z * 2 + core) * 8 + head]
        locs = []
        for j in range(SPANS):
            d = spans_ref[j, seg]
            away = ((d // 2) % 8 - z) & 7
            locs.append(away * 4 + (((d // 16) * 2 + d % 2) ^ quad))
        q, do = qd_ref[u, :, :HEAD_DIM], qd_ref[u, :, HEAD_DIM:]
        keys = jnp.concatenate([k_ref[loc] for loc in locs], axis=0)
        scores = nt(keys, q)
        values = jnp.concatenate([v_ref[loc] for loc in locs], axis=0)
        yield
        dprob = nt(values, do)
        top = jnp.max(scores, axis=0, keepdims=True)
        expo = jnp.exp2((scores - top) * (FACTOR * LOG2E))
        prob = expo * (1.0 / jnp.sum(expo, axis=0, keepdims=True))
        prob_b = prob.astype(BF16)
        value_t = jnp.concatenate([vt_ref[loc] for loc in locs], axis=1)
        yield
        attn_t = nn(value_t, prob_b)
        yield
        value_slots = nn(prob_b, do)
        od_ref[u, :, :HEAD_DIM] = attn_t.T.astype(BF16)
        delta = jnp.sum(do.astype(F32).T * attn_t, axis=0, keepdims=True)
        dscore_b = (prob * (dprob - delta)).astype(BF16)
        key_t = jnp.concatenate([kt_ref[loc] for loc in locs], axis=1)
        yield
        dq_t = nn(key_t, dscore_b) * FACTOR
        key_slots = nn(dscore_b, q)
        yield
        od_ref[u, :, HEAD_DIM:] = dq_t.T.astype(BF16)
        for j in range(SPANS):
            rows = slice(j * BLOCK, (j + 1) * BLOCK)
            dk_ref[locs[j]] += key_slots[rows]
            dv_ref[locs[j]] += value_slots[rows]

    live = [one_block(u) for u in range(UNROLL)]
    while live:
        live = [block for block in live if next(block, True) is None]

    @pl.when(pl.program_id(0) == pl.num_programs(0) - 1)
    def _():
        for o in range(PLANES):

            @pl.loop(0, 4)
            def _(t):
                key_parts[o][t] = (dk_ref[4 * o + t] * FACTOR).astype(BF16)
                value_parts[o][t] = dv_ref[4 * o + t].astype(BF16)


def attention(me, seg_map, spans_t, qd, keys, values):
    cad_blocks, doc_blocks = qd.shape[0], 4 * PLANES
    step = pl.BlockSpec((UNROLL, BLOCK, WIDE), lambda i: (i, 0, 0))
    square = (doc_blocks, BLOCK, HEAD_DIM)
    od, *parts = call(
        attention_kernel,
        "attention",
        [SMEM] * 3 + [step] + [VMEM] * 2 * PLANES,
        [qd.shape] + [(4, BLOCK, HEAD_DIM)] * 2 * PLANES,
        [pltpu.VMEM(square, BF16)] * 4 + [pltpu.VMEM(square, F32)] * 2,
        [step] + [VMEM] * 2 * PLANES,
        grid=(cad_blocks // UNROLL,),
        cost_estimate=pl.CostEstimate(
            flops=cad_blocks * SPANS * 12 * BLOCK * BLOCK * HEAD_DIM,
            bytes_accessed=2 * (2 * qd.size + 4 * doc_blocks * BLOCK * HEAD_DIM),
            transcendentals=cad_blocks * SPANS * BLOCK * BLOCK,
        ),
    )(me, seg_map, spans_t, qd, *keys, *values)
    return od, parts[:PLANES], parts[PLANES:]


def up(array):
    return lax.ppermute(array, "z", [(i, (i + 1) % PLANES) for i in range(PLANES)])


def down(array):
    return lax.ppermute(array, "z", [(i, (i - 1) % PLANES) for i in range(PLANES)])


def exchange(tiles):
    return [tiles[0]] + [
        lax.ppermute(tiles[t], QUAD, [(i, i ^ t) for i in range(4)]) for t in (1, 2, 3)
    ]


def relay(own, move, steps):
    held = [own]
    for _ in range(steps):
        held.append(move(held[-1]))
    return held


def gather_z(own, ups):
    rising, falling = relay(own, up, ups), relay(own, down, PLANES - 1 - ups)
    return falling + rising[:0:-1]


def collect(parts, move):
    total = move(parts[0])
    for part in parts[1:]:
        total = move(plus(part, total))
    return total


def scatter_z(parts, ups):
    return parts[0], collect(parts[ups:0:-1], up), collect(parts[ups + 1 :], down)


def swap(array):
    return lax.all_to_all(array, PLANE, split_axis=0, concat_axis=0, tiled=True)


def body(query, key, value, d_out, seg_map, spans):
    me = jnp.stack([lax.axis_index(QUAD), lax.axis_index("z")]).astype(jnp.int32)
    tiles = exchange(split_kv(me, key, value))
    qd, tiles = lax.optimization_barrier((split_heads(query, d_out), tiles))
    own_keys = jnp.stack([tile[:, :HEAD_DIM] for tile in tiles])
    own_values = jnp.stack([tile[:, HEAD_DIM:] for tile in tiles])
    qd, keys, values = swap(qd), gather_z(own_keys, 4), gather_z(own_values, 3)
    od, key_parts, value_parts = attention(me, seg_map, spans.T, qd, keys, values)
    od = swap(od)
    sums = scatter_z(key_parts, 4), scatter_z(value_parts, 3)
    tiles = [jnp.concatenate([plus(*(x[t] for x in s)) for s in sums], axis=1) for t in range(4)]
    od, tiles = lax.optimization_barrier((od, tiles))
    attn_out, d_query = join_heads(od)
    d_key, d_value = join_kv(me, exchange(tiles))
    return attn_out, d_query, d_key, d_value


def solution(mesh):
    fine = Mesh(mesh.devices.reshape(2, PLANES, 2, 8), ("xhi", "z", "core", "head"))
    blk = ("xhi", "z", "core")
    rows, tiles = P((*blk, "head"), None), P(blk, "head")
    return jax.shard_map(
        body,
        mesh=fine,
        in_specs=(rows, tiles, tiles, rows, P(), P()),
        out_specs=(rows, rows, tiles, tiles),
        check_vma=False,
    )
```

```python
import math

import jax
import jax.numpy as jnp
from jax import lax
from jax.experimental import pallas as pl
from jax.experimental.pallas import tpu as pltpu
from jax.sharding import Mesh, PartitionSpec as P

HEAD_DIM = 128
BLOCK = 128
SPANS = 8
PLANES = 8
PLANE = ("head", "xhi", "core")
QUAD = ("xhi", "core")
FACTOR = 1.0 / math.sqrt(HEAD_DIM)
LOG2E = math.log2(math.e)
UNROLL = 8
VMEM_MIB, SMALL_MIB = 60, 8
WIDE = 2 * HEAD_DIM
BF16, F32 = jnp.bfloat16, jnp.float32
SMEM = pl.BlockSpec(memory_space=pltpu.SMEM)
VMEM = pl.BlockSpec(memory_space=pltpu.VMEM)


def nt(a, b):
    return lax.dot_general(a, b, (((1,), (1,)), ((), ())), preferred_element_type=F32)


def nn(a, b):
    return lax.dot_general(a, b, (((1,), (0,)), ((), ())), preferred_element_type=F32)


def columns(block):
    return pl.ds(pl.multiple_of(block * HEAD_DIM, HEAD_DIM), HEAD_DIM)


def call(kernel, name, in_specs, shapes, scratch=(), out_specs=None, **params):
    return pl.pallas_call(
        kernel,
        out_shape=tuple(jax.ShapeDtypeStruct(shape, BF16) for shape in shapes),
        in_specs=in_specs,
        out_specs=tuple(out_specs or [VMEM for _ in shapes]),
        scratch_shapes=scratch,
        name=name,
        compiler_params=pltpu.CompilerParams(vmem_limit_bytes=(SMALL_MIB if name.startswith("join") else VMEM_MIB) * 2**20),
        **params,
    )


def split_kv(key, value):
    def kernel(key_ref, value_ref, *tiles):
        quad = lax.axis_index(QUAD)
        for t, tile in enumerate(tiles):
            tile[:, :HEAD_DIM] = key_ref[:, columns(quad ^ t)]
            tile[:, HEAD_DIM:] = value_ref[:, columns(quad ^ t)]

    return call(kernel, "split_kv", [VMEM, VMEM], [(BLOCK, WIDE)] * 4)(key, value)


def join_kv(tiles):
    def kernel(*refs):
        quad = lax.axis_index(QUAD)
        *tiles, key_ref, value_ref = refs
        for t, tile in enumerate(tiles):
            key_ref[:, columns(quad ^ t)] = tile[:, :HEAD_DIM]
            value_ref[:, columns(quad ^ t)] = tile[:, HEAD_DIM:]

    return call(kernel, "join_kv", [VMEM] * 4, [(BLOCK, 4 * HEAD_DIM)] * 2)(*tiles)


def split_heads(query, d_out):
    heads = query.shape[1] // HEAD_DIM

    def kernel(query_ref, d_out_ref, tiles):
        for h in range(heads):
            tiles[h, :, :HEAD_DIM] = query_ref[:, columns(h)]
            tiles[h, :, HEAD_DIM:] = d_out_ref[:, columns(h)]

    return call(kernel, "split_heads", [VMEM] * 2, [(heads, BLOCK, WIDE)])(query, d_out)[0]


def join_heads(tiles):
    heads = tiles.shape[0]

    def kernel(tiles, attn_ref, grad_ref):
        for h in range(heads):
            attn_ref[:, columns(h)] = tiles[h, :, :HEAD_DIM]
            grad_ref[:, columns(h)] = tiles[h, :, HEAD_DIM:]

    return call(kernel, "join_heads", [VMEM], [(BLOCK, heads * HEAD_DIM)] * 2)(tiles)


def plus(*terms):
    return sum(term.astype(F32) for term in terms).astype(BF16)


def attention_kernel(seg_ref, spans_ref, qd_ref, *refs):
    keys_in, values_in, od_ref = refs[:PLANES], refs[PLANES : 2 * PLANES], refs[2 * PLANES]
    key_parts, value_parts = refs[2 * PLANES + 1 : 3 * PLANES + 1], refs[3 * PLANES + 1 : 4 * PLANES + 1]
    k_ref, v_ref, kt_ref, vt_ref, dk_ref, dv_ref = refs[4 * PLANES + 1 :]
    quad, z = lax.axis_index(QUAD), lax.axis_index("z")

    @pl.when(pl.program_id(0) == 0)
    def _():
        for o in range(PLANES):

            @pl.loop(0, 4, unroll=True)
            def _(t):
                for piece, held, turned, total in (
                    (keys_in[o], k_ref, kt_ref, dk_ref),
                    (values_in[o], v_ref, vt_ref, dv_ref),
                ):
                    tile = piece[t]
                    held[4 * o + t] = tile
                    turned[4 * o + t] = tile.T
                    total[4 * o + t] = jnp.zeros((BLOCK, HEAD_DIM), F32)

    def one_block(u):
        s = pl.program_id(0) * UNROLL + u
        head, xhi, core = s // 4, (s // 2) % 2, s % 2
        seg = seg_ref[(xhi * 16 + z * 2 + core) * 8 + head]
        locs = []
        for j in range(SPANS):
            d = spans_ref[j, seg]
            away = ((d // 2) % 8 - z) & 7
            locs.append(away * 4 + (((d // 16) * 2 + d % 2) ^ quad))
        q, do = qd_ref[u, :, :HEAD_DIM], qd_ref[u, :, HEAD_DIM:]
        keys = jnp.concatenate([k_ref[loc] for loc in locs], axis=0)
        scores = nt(keys, q)
        values = jnp.concatenate([v_ref[loc] for loc in locs], axis=0)
        yield
        top = jnp.max(scores, axis=0, keepdims=True)
        expo = jnp.exp2((scores - top) * (FACTOR * LOG2E))
        prob = expo * (1.0 / jnp.sum(expo, axis=0, keepdims=True))
        prob_b = prob.astype(BF16)
        value_t = jnp.concatenate([vt_ref[loc] for loc in locs], axis=1)
        yield
        attn_t = nn(value_t, prob_b)
        dprob = nt(values, do)
        value_slots = nn(prob_b, do)
        for j in range(SPANS):
            dv_ref[locs[j]] += value_slots[j * BLOCK : (j + 1) * BLOCK]
        yield
        od_ref[u, :, :HEAD_DIM] = attn_t.T.astype(BF16)
        delta = jnp.sum(do.astype(F32).T * attn_t, axis=0, keepdims=True)
        dscore_b = (prob * (dprob - delta)).astype(BF16)
        key_t = jnp.concatenate([kt_ref[loc] for loc in locs], axis=1)
        yield
        dq_t = nn(key_t, dscore_b) * FACTOR
        key_slots = nn(dscore_b, q)
        yield
        od_ref[u, :, HEAD_DIM:] = dq_t.T.astype(BF16)
        for j in range(SPANS):
            rows = slice(j * BLOCK, (j + 1) * BLOCK)
            dk_ref[locs[j]] += key_slots[rows]

    live = [one_block(u) for u in range(UNROLL)]
    while live:
        live = [block for block in live if next(block, True) is None]

    @pl.when(pl.program_id(0) == pl.num_programs(0) - 1)
    def _():
        for o in range(PLANES):

            @pl.loop(0, 4)
            def _(t):
                key_parts[o][t] = (dk_ref[4 * o + t] * FACTOR).astype(BF16)
                value_parts[o][t] = dv_ref[4 * o + t].astype(BF16)


def attention(seg_map, spans_t, qd, keys, values):
    cad_blocks, doc_blocks = qd.shape[0], 4 * PLANES
    step = pl.BlockSpec((UNROLL, BLOCK, WIDE), lambda i: (i, 0, 0))
    square = (doc_blocks, BLOCK, HEAD_DIM)
    od, *parts = call(
        attention_kernel,
        "attention",
        [SMEM] * 2 + [step] + [VMEM] * 2 * PLANES,
        [qd.shape] + [(4, BLOCK, HEAD_DIM)] * 2 * PLANES,
        [pltpu.VMEM(square, BF16)] * 4 + [pltpu.VMEM(square, F32)] * 2,
        [step] + [VMEM] * 2 * PLANES,
        grid=(cad_blocks // UNROLL,),
        cost_estimate=pl.CostEstimate(
            flops=cad_blocks * SPANS * 12 * BLOCK * BLOCK * HEAD_DIM,
            bytes_accessed=2 * (2 * qd.size + 4 * doc_blocks * BLOCK * HEAD_DIM),
            transcendentals=cad_blocks * SPANS * BLOCK * BLOCK,
        ),
    )(seg_map, spans_t, qd, *keys, *values)
    return od, parts[:PLANES], parts[PLANES:]


def up(array):
    return lax.ppermute(array, "z", [(i, (i + 1) % PLANES) for i in range(PLANES)])


def down(array):
    return lax.ppermute(array, "z", [(i, (i - 1) % PLANES) for i in range(PLANES)])


def exchange(tiles):
    return [tiles[0]] + [
        lax.ppermute(tiles[t], QUAD, [(i, i ^ t) for i in range(4)]) for t in (1, 2, 3)
    ]


def relay(own, move, steps):
    held = [own]
    for _ in range(steps):
        held.append(move(held[-1]))
    return held


def gather_z(own, ups):
    rising, falling = relay(own, up, ups), relay(own, down, PLANES - 1 - ups)
    return falling + rising[:0:-1]


def collect(parts, move):
    total = move(parts[0])
    for part in parts[1:]:
        total = move(plus(part, total))
    return total


def scatter_z(parts, ups):
    return parts[0], collect(parts[ups:0:-1], up), collect(parts[ups + 1 :], down)


def swap(array):
    return lax.all_to_all(array, PLANE, split_axis=0, concat_axis=0, tiled=True)


def body(query, key, value, d_out, seg_map, spans):
    tiles = exchange(split_kv(key, value))
    qd, tiles = lax.optimization_barrier((split_heads(query, d_out), tiles))
    own_keys = jnp.stack([tile[:, :HEAD_DIM] for tile in tiles])
    own_values = jnp.stack([tile[:, HEAD_DIM:] for tile in tiles])
    qd, keys, values = swap(qd), gather_z(own_keys, 4), gather_z(own_values, 3)
    od, key_parts, value_parts = attention(seg_map, spans.T, qd, keys, values)
    od = swap(od)
    sums = scatter_z(key_parts, 4), scatter_z(value_parts, 3)
    tiles = [jnp.concatenate([plus(*(x[t] for x in s)) for s in sums], axis=1) for t in range(4)]
    od, tiles = lax.optimization_barrier((od, tiles))
    attn_out, d_query = join_heads(od)
    d_key, d_value = join_kv(exchange(tiles))
    return attn_out, d_query, d_key, d_value


def solution(mesh):
    fine = Mesh(mesh.devices.reshape(2, PLANES, 2, 8), ("xhi", "z", "core", "head"))
    blk = ("xhi", "z", "core")
    rows, tiles = P((*blk, "head"), None), P(blk, "head")
    return jax.shard_map(
        body,
        mesh=fine,
        in_specs=(rows, tiles, tiles, rows, P(), P()),
        out_specs=(rows, rows, tiles, tiles),
        check_vma=False,
    )
```

```python
import math

import jax
import jax.numpy as jnp
from jax import lax
from jax.experimental import pallas as pl
from jax.experimental.pallas import tpu as pltpu
from jax.sharding import Mesh, PartitionSpec as P

HEAD_DIM = 128
BLOCK = 128
SPANS = 8
PLANES = 8
PLANE = ("head", "xhi", "core")
QUAD = ("xhi", "core")
FACTOR = 1.0 / math.sqrt(HEAD_DIM)
LOG2E = math.log2(math.e)
UNROLL = 8
VMEM_MIB, SMALL_MIB = 60, 8
WIDE = 2 * HEAD_DIM
BF16, F32 = jnp.bfloat16, jnp.float32
SMEM = pl.BlockSpec(memory_space=pltpu.SMEM)
VMEM = pl.BlockSpec(memory_space=pltpu.VMEM)


def nt(a, b):
    return lax.dot_general(a, b, (((1,), (1,)), ((), ())), preferred_element_type=F32)


def nn(a, b):
    return lax.dot_general(a, b, (((1,), (0,)), ((), ())), preferred_element_type=F32)


def columns(block):
    return pl.ds(pl.multiple_of(block * HEAD_DIM, HEAD_DIM), HEAD_DIM)


def call(kernel, name, in_specs, shapes, scratch=(), out_specs=None, **params):
    return pl.pallas_call(
        kernel,
        out_shape=tuple(jax.ShapeDtypeStruct(shape, BF16) for shape in shapes),
        in_specs=in_specs,
        out_specs=tuple(out_specs or [VMEM for _ in shapes]),
        scratch_shapes=scratch,
        name=name,
        compiler_params=pltpu.CompilerParams(vmem_limit_bytes=(SMALL_MIB if name.startswith("join") else VMEM_MIB) * 2**20),
        **params,
    )


def split_kv(key, value):
    def kernel(key_ref, value_ref, *tiles):
        quad = lax.axis_index(QUAD)
        for t, tile in enumerate(tiles):
            tile[:, :HEAD_DIM] = key_ref[:, columns(quad ^ t)]
            tile[:, HEAD_DIM:] = value_ref[:, columns(quad ^ t)]

    return call(kernel, "split_kv", [VMEM, VMEM], [(BLOCK, WIDE)] * 4)(key, value)


def join_kv(tiles):
    def kernel(*refs):
        quad = lax.axis_index(QUAD)
        *tiles, key_ref, value_ref = refs
        for t, tile in enumerate(tiles):
            key_ref[:, columns(quad ^ t)] = tile[:, :HEAD_DIM]
            value_ref[:, columns(quad ^ t)] = tile[:, HEAD_DIM:]

    return call(kernel, "join_kv", [VMEM] * 4, [(BLOCK, 4 * HEAD_DIM)] * 2)(*tiles)


def split_heads(query, d_out):
    heads = query.shape[1] // HEAD_DIM

    def kernel(query_ref, d_out_ref, tiles):
        for h in range(heads):
            tiles[h, :, :HEAD_DIM] = query_ref[:, columns(h)]
            tiles[h, :, HEAD_DIM:] = d_out_ref[:, columns(h)]

    return call(kernel, "split_heads", [VMEM] * 2, [(heads, BLOCK, WIDE)])(query, d_out)[0]


def join_heads(tiles):
    heads = tiles.shape[0]

    def kernel(tiles, attn_ref, grad_ref):
        for h in range(heads):
            attn_ref[:, columns(h)] = tiles[h, :, :HEAD_DIM]
            grad_ref[:, columns(h)] = tiles[h, :, HEAD_DIM:]

    return call(kernel, "join_heads", [VMEM], [(BLOCK, heads * HEAD_DIM)] * 2)(tiles)


def plus(*terms):
    return sum(term.astype(F32) for term in terms).astype(BF16)


def attention_kernel(seg_ref, spans_ref, qd_ref, *refs):
    keys_in, values_in, od_ref = refs[:PLANES], refs[PLANES : 2 * PLANES], refs[2 * PLANES]
    key_parts, value_parts = refs[2 * PLANES + 1 : 3 * PLANES + 1], refs[3 * PLANES + 1 : 4 * PLANES + 1]
    k_ref, v_ref, kt_ref, vt_ref, dk_ref, dv_ref = refs[4 * PLANES + 1 :]
    quad, z = lax.axis_index(QUAD), lax.axis_index("z")

    @pl.when(pl.program_id(0) == 0)
    def _():
        for o in range(PLANES):

            @pl.loop(0, 4, unroll=True)
            def _(t):
                for piece, held, turned, total in (
                    (keys_in[o], k_ref, kt_ref, dk_ref),
                    (values_in[o], v_ref, vt_ref, dv_ref),
                ):
                    tile = piece[t]
                    held[4 * o + t] = tile
                    turned[4 * o + t] = tile.T
                    total[4 * o + t] = jnp.zeros((BLOCK, HEAD_DIM), F32)

    def one_block(u):
        s = pl.program_id(0) * UNROLL + u
        head, xhi, core = s // 4, (s // 2) % 2, s % 2
        seg = seg_ref[(xhi * 16 + z * 2 + core) * 8 + head]
        locs = []
        for j in range(SPANS):
            d = spans_ref[j, seg]
            away = ((d // 2) % 8 - z) & 7
            locs.append(away * 4 + (((d // 16) * 2 + d % 2) ^ quad))
        q, do = qd_ref[u, :, :HEAD_DIM], qd_ref[u, :, HEAD_DIM:]
        keys = jnp.concatenate([k_ref[loc] for loc in locs], axis=0)
        scores = nt(keys, q)
        values = jnp.concatenate([v_ref[loc] for loc in locs], axis=0)
        yield
        top = jnp.max(scores, axis=0, keepdims=True)
        expo = jnp.exp2((scores - top) * (FACTOR * LOG2E))
        prob = expo * (1.0 / jnp.sum(expo, axis=0, keepdims=True))
        prob_b = prob.astype(BF16)
        value_t = jnp.concatenate([vt_ref[loc] for loc in locs], axis=1)
        yield
        attn_t = nn(value_t, prob_b)
        dprob = nt(values, do)
        value_slots = nn(prob_b, do)
        for j in range(SPANS):
            dv_ref[locs[j]] += value_slots[j * BLOCK : (j + 1) * BLOCK]
        yield
        od_ref[u, :, :HEAD_DIM] = attn_t.T.astype(BF16)
        delta = jnp.sum(do.astype(F32).T * attn_t, axis=0, keepdims=True)
        dscore_b = (prob * (dprob - delta)).astype(BF16)
        key_t = jnp.concatenate([kt_ref[loc] for loc in locs], axis=1)
        yield
        key_slots = nn(dscore_b, q)
        dq_t = nn(key_t, dscore_b) * FACTOR
        yield
        od_ref[u, :, HEAD_DIM:] = dq_t.T.astype(BF16)
        for j in range(SPANS):
            rows = slice(j * BLOCK, (j + 1) * BLOCK)
            dk_ref[locs[j]] += key_slots[rows]

    live = [one_block(u) for u in range(UNROLL)]
    while live:
        live = [block for block in live if next(block, True) is None]

    @pl.when(pl.program_id(0) == pl.num_programs(0) - 1)
    def _():
        for o in range(PLANES):

            @pl.loop(0, 4)
            def _(t):
                key_parts[o][t] = (dk_ref[4 * o + t] * FACTOR).astype(BF16)
                value_parts[o][t] = dv_ref[4 * o + t].astype(BF16)


def attention(seg_map, spans_t, qd, keys, values):
    cad_blocks, doc_blocks = qd.shape[0], 4 * PLANES
    step = pl.BlockSpec((UNROLL, BLOCK, WIDE), lambda i: (i, 0, 0))
    square = (doc_blocks, BLOCK, HEAD_DIM)
    od, *parts = call(
        attention_kernel,
        "attention",
        [SMEM] * 2 + [step] + [VMEM] * 2 * PLANES,
        [qd.shape] + [(4, BLOCK, HEAD_DIM)] * 2 * PLANES,
        [pltpu.VMEM(square, BF16)] * 4 + [pltpu.VMEM(square, F32)] * 2,
        [step] + [VMEM] * 2 * PLANES,
        grid=(cad_blocks // UNROLL,),
        cost_estimate=pl.CostEstimate(
            flops=cad_blocks * SPANS * 12 * BLOCK * BLOCK * HEAD_DIM,
            bytes_accessed=2 * (2 * qd.size + 4 * doc_blocks * BLOCK * HEAD_DIM),
            transcendentals=cad_blocks * SPANS * BLOCK * BLOCK,
        ),
    )(seg_map, spans_t, qd, *keys, *values)
    return od, parts[:PLANES], parts[PLANES:]


def up(array):
    return lax.ppermute(array, "z", [(i, (i + 1) % PLANES) for i in range(PLANES)])


def down(array):
    return lax.ppermute(array, "z", [(i, (i - 1) % PLANES) for i in range(PLANES)])


def exchange(tiles):
    return [tiles[0]] + [
        lax.ppermute(tiles[t], QUAD, [(i, i ^ t) for i in range(4)]) for t in (1, 2, 3)
    ]


def relay(own, move, steps):
    held = [own]
    for _ in range(steps):
        held.append(move(held[-1]))
    return held


def gather_z(own, ups):
    rising, falling = relay(own, up, ups), relay(own, down, PLANES - 1 - ups)
    return falling + rising[:0:-1]


def collect(parts, move):
    total = move(parts[0])
    for part in parts[1:]:
        total = move(plus(part, total))
    return total


def scatter_z(parts, ups):
    return parts[0], collect(parts[ups:0:-1], up), collect(parts[ups + 1 :], down)


def swap(array):
    return lax.all_to_all(array, PLANE, split_axis=0, concat_axis=0, tiled=True)


def body(query, key, value, d_out, seg_map, spans):
    tiles = exchange(split_kv(key, value))
    qd, tiles = lax.optimization_barrier((split_heads(query, d_out), tiles))
    own_keys = jnp.stack([tile[:, :HEAD_DIM] for tile in tiles])
    own_values = jnp.stack([tile[:, HEAD_DIM:] for tile in tiles])
    qd, keys, values = swap(qd), gather_z(own_keys, 4), gather_z(own_values, 3)
    od, key_parts, value_parts = attention(seg_map, spans.T, qd, keys, values)
    od = swap(od)
    sums = scatter_z(key_parts, 4), scatter_z(value_parts, 3)
    tiles = [jnp.concatenate([plus(*(x[t] for x in s)) for s in sums], axis=1) for t in range(4)]
    od, tiles = lax.optimization_barrier((od, tiles))
    attn_out, d_query = join_heads(od)
    d_key, d_value = join_kv(exchange(tiles))
    return attn_out, d_query, d_key, d_value


def solution(mesh):
    fine = Mesh(mesh.devices.reshape(2, PLANES, 2, 8), ("xhi", "z", "core", "head"))
    blk = ("xhi", "z", "core")
    rows, tiles = P((*blk, "head"), None), P(blk, "head")
    return jax.shard_map(
        body,
        mesh=fine,
        in_specs=(rows, tiles, tiles, rows, P(), P()),
        out_specs=(rows, rows, tiles, tiles),
        check_vma=False,
    )
```
